32 devices in a mesh: grp: 2 (over x), row: 8 (over z, y), col: 2 (over core).
Axes of the slice: x: 2, y: 2, z: 4, core: 2. Of those that a mesh axis runs over, the one named last changes fastest.
Arguments:
- tiles: bfloat16 [1024, 512, 512], P(('grp', 'row', 'col')), parts along dimension 0, may hold values from -0.25 to 0.25
- tile_row: int32 [1024], P(('grp', 'row', 'col')), parts along dimension 0, may hold values from 0 to 31, as said below
- tile_col: int32 [1024], P(('grp', 'row', 'col')), parts along dimension 0, may hold values from 0 to 31, as said below
- counts: int32 [32], P(('grp', 'row', 'col')), parts along dimension 0, may hold values from 10 to 32, as said below
- start: float32 [32768, 64], P(('grp', 'row', 'col')), parts along dimension 0, may hold values from -6 to 6
Outputs:
- basis: float32 [32768, 64], P(('grp', 'row', 'col')), parts along dimension 0
- ritz: float32 [6, 64, 64], P('grp'), parts along dimension 0
The draws below stay inside these ranges and needn't reach their ends.
There are 2 independent parts, one for each index of `grp`. The reference program is written for one: setup_inputs(seed, part) draws one part's arguments, and reference() takes and returns one part's arrays. A program takes and returns all parts, laid end to end along the dimension named above; each array names one. Nothing has to cross between parts.
Inputs may be any that keep to these rules, and one draw needn't show every extreme that they name: `tile_row`: slot s lies on device d = s // 32 = r * 2 + c; its tile row is in r * 2 * 2 to (r + 1) * 2 * 2 - 1, and its tile column j has (j // 2) % 2 == c. `tile_col`: see tile_row for which tile columns a device holds. `counts`: some device is full in every draw.
All inputs are finite; a program needn't handle non-finite values.
Results may differ from the reference program's by a relative error of at most 0.0055.
Values may be sent and summed in bfloat16 or wider, within the bound.
A program may use at most 64 MiB of HBM per device.

```python
import jax
import jax.numpy as jnp
from jax import lax

TILE = 512
K = 64
TB = 2
TILES_DEV = 32
ITERS = 3
NODES = 16384
TILES = 512
N_ROW = 8
N_COL = 2


def draw_tile_row(key, part):
    key = jax.random.fold_in(key, 11)
    device = jnp.arange(TILES, dtype=jnp.int32) // TILES_DEV
    band = device // N_COL
    offset = jax.random.randint(key, (TILES,), 0, N_COL * TB, dtype=jnp.int32)
    return band * N_COL * TB + offset


def draw_tile_col(key, part):
    key = jax.random.fold_in(key, 23)
    first, second = jax.random.split(key)
    device = jnp.arange(TILES, dtype=jnp.int32) // TILES_DEV
    column_class = device % N_COL
    source = jax.random.randint(first, (TILES,), 0, N_ROW, dtype=jnp.int32)
    inner = jax.random.randint(second, (TILES,), 0, TB, dtype=jnp.int32)
    return (source * N_COL + column_class) * TB + inner


def draw_counts(key, part):
    key = jax.random.fold_in(key, 37)
    first, second = jax.random.split(key)
    devices = N_ROW * N_COL
    base = jax.random.randint(first, (devices,), TILES_DEV // 3, 2 * TILES_DEV // 3 + 1, dtype=jnp.int32)
    heavy = jax.random.randint(second, (), 0, devices, dtype=jnp.int32)
    return jnp.where(jnp.arange(devices, dtype=jnp.int32) == heavy, TILES_DEV, base).astype(jnp.int32)


def levels(own_key, extent, shards, least, top_value):
    def one(axis_at, shards_of):
        draws = jax.random.uniform(jax.random.fold_in(jax.random.fold_in(own_key, 6), axis_at), (shards_of,), jnp.float32, least / len(shards), top_value / len(shards))
        return jnp.repeat(jnp.exp(draws), extent[axis_at] // shards_of).reshape((-1,) + (1,) * (len(extent) - axis_at - 1))

    level = one(*shards[0])
    for cut in shards[1:]:
        level = level * one(*cut)
    return level


def normal_values(own_key, shape, width, most, pieces=(), kind=jnp.bfloat16):
    values = jax.random.normal(own_key, shape, jnp.float32) * width
    if len(pieces) > 0:
        values = levels(own_key, shape, pieces, -0.22, 0.18) * values
    return jnp.clip(values, min=-most, max=most).astype(kind)


def setup_inputs(seed: int = 0, part: int = 0) -> dict:
    key_of = jax.random.split(jax.random.key(seed), 6)
    own_keys = jax.random.split(jax.random.fold_in(key_of[5], part), 6)
    return {
        "tiles": normal_values(own_keys[0], (TILES, TILE, TILE), ((TILE * TILES_DEV // 4) ** -0.5), 0.25, ((0, 16),)),
        "tile_row": draw_tile_row(jax.random.fold_in(jax.random.fold_in(key_of[5], part), 71), part),
        "tile_col": draw_tile_col(jax.random.fold_in(jax.random.fold_in(key_of[5], part), 71), part),
        "counts": draw_counts(jax.random.fold_in(jax.random.fold_in(key_of[5], part), 71), part),
        "start": normal_values(own_keys[4], (NODES, K), 1.0, 6.0, ((0, 16),), jnp.float32),
    }


def reference(tiles, tile_row, tile_col, counts, start):
    slots = jnp.arange(TILES, dtype=jnp.int32)
    owner = slots // TILES_DEV
    live = (slots % TILES_DEV < counts[owner]).astype(jnp.float32)
    blocks = NODES // TILE
    basis = start
    quotients = []
    for step in range(ITERS):
        low = basis.astype(jnp.bfloat16).reshape(blocks, TILE, K)

        def add_tile(acc, item):
            tile, row_id, col_id, weight = item
            piece = lax.dynamic_index_in_dim(low, col_id, 0, keepdims=False)
            prod = jnp.dot(tile.astype(jnp.float32), piece.astype(jnp.float32), preferred_element_type=jnp.float32) * weight
            old = lax.dynamic_index_in_dim(acc, row_id, 0, keepdims=False)
            return (lax.dynamic_update_index_in_dim(acc, old + prod, row_id, 0), None)
        image, unused = lax.scan(add_tile, jnp.zeros((blocks, TILE, K), jnp.float32), (tiles, tile_row, tile_col, live))
        image = image.reshape(NODES, K)
        gram = jnp.dot(image.T, image, precision=lax.Precision.HIGHEST) / NODES
        quotients.append(jnp.dot(basis.T, image, precision=lax.Precision.HIGHEST) / jnp.sqrt(jnp.float32(NODES)))
        lower = jnp.linalg.cholesky(gram)
        basis = jax.scipy.linalg.solve_triangular(lower, image.T, lower=True).T
    return (basis, jnp.stack(quotients))
```

```python
import functools

import jax
import jax.numpy as jnp
from jax import lax
from jax.experimental import pallas as pl
from jax.experimental.pallas import tpu as pltpu
from jax.sharding import PartitionSpec as P

TILE = 512
ITERS = 3
MESH = pl.DeviceIdType.MESH
EXACT = lax.Precision.HIGHEST
NT = (((1,), (1,)), ((), ()))
LOADS = 4


def pack(square):
    half = square.shape[0] // 2
    return jnp.concatenate([square[:half], square[half:]], axis=1)


def unpack(packed):
    half = packed.shape[1] // 2
    return jnp.concatenate([packed[:, :half], packed[:, half:]], axis=0)


def inverse_factor(gram, work, scale):
    width = gram.shape[0]
    lanes = 2 * width
    rows = lax.broadcasted_iota(jnp.int32, (width, lanes), 0)
    columns = lax.broadcasted_iota(jnp.int32, (width, lanes), 1)
    rows8 = lax.broadcasted_iota(jnp.int32, (8, lanes), 0)
    eye = (rows + width == columns).astype(jnp.float32)
    padded = jnp.concatenate([gram, jnp.zeros_like(gram)], axis=1)
    work[...] = padded + eye

    def body(block, carry):
        whole = work[...]
        first = pl.multiple_of(block * 8, 8)
        here = work[pl.ds(first, 8), :]
        below = rows - first
        cols = [jnp.broadcast_to(whole[:, q : q + 1], (width, lanes)) for q in range(8)]
        cols8 = [jnp.broadcast_to(here[:, q : q + 1], (8, lanes)) for q in range(8)]
        pivots = jnp.ones((8, lanes), jnp.float32)
        for p in range(8):
            inverse = 1.0 / cols8[p][p : p + 1, :]
            pivots = jnp.where(rows8 == p, inverse, pivots)
            factor = jnp.where(below > p, cols[p] * inverse, 0.0)
            factor8 = jnp.where(rows8 > p, cols8[p] * inverse, 0.0)
            pivot_row = here[p : p + 1, :]
            for q in range(p + 1, 8):
                entry = cols8[q][p : p + 1, :]
                cols[q] = cols[q] - factor * entry
                cols8[q] = cols8[q] - factor8 * entry
            here = here - factor8 * pivot_row
            whole = whole - factor * pivot_row
        scale[pl.ds(first, 8), :] = pivots
        work[...] = pltpu.roll(whole, lanes - 8, 1)
        return carry

    lax.fori_loop(0, width // 8, body, 0)
    return (work[...] * jnp.sqrt(scale[...]))[:, :width]


def kernel(
    row_count,
    y_count,
    nodes,
    tiles_hbm,
    row_ref,
    col_ref,
    count_ref,
    start_ref,
    basis_ref,
    ritz_ref,
    tiles,
    gathered,
    partial,
    crossed,
    image,
    iterate,
    core_sum,
    y_sum,
    z_sum,
    rit_core,
    rit_y,
    rit_z,
    work,
    scale,
    load_sem,
    low_recv,
    low_up,
    low_down,
    low_over,
    cross_send,
    cross_recv,
    core_send,
    core_recv,
    y_send,
    y_recv,
    z_send,
    z_recv,
):
    z_count = row_count // y_count
    me = lax.axis_index("row")
    core = lax.axis_index("col")
    here_z = me // y_count
    here_y = me % y_count
    blocks = iterate.shape[0]
    width = iterate.shape[1]
    slots = tiles.shape[0]
    band = partial.shape[0]
    sibling = {"col": 1 - core}
    over = {"row": here_z * y_count + (1 - here_y)}

    chunk = slots // LOADS
    loads = [
        pltpu.make_async_copy(
            tiles_hbm.at[pl.ds(i * chunk, chunk)],
            tiles.at[pl.ds(i * chunk, chunk)],
            load_sem.at[i],
        )
        for i in range(LOADS)
    ]
    for load in loads:
        load.start()

    barrier = pltpu.get_barrier_semaphore()
    pl.semaphore_signal(barrier, inc=1, device_id=sibling, device_id_type=MESH)
    if y_count > 1:
        pl.semaphore_signal(barrier, inc=1, device_id=over, device_id_type=MESH)
    for step in range(1, z_count):
        other = lax.rem(here_z + step, z_count) * y_count + here_y
        pl.semaphore_signal(barrier, inc=1, device_id={"row": other}, device_id_type=MESH)

    for b in range(blocks):
        iterate[b] = start_ref[b * TILE : (b + 1) * TILE, :].T
        gathered[0, me * blocks + b] = iterate[b].astype(jnp.bfloat16)
    pl.semaphore_wait(barrier, z_count - 1 + (1 if y_count > 1 else 0) + 1)

    def low_copy(k, source, send_sem, device_id):
        part = gathered.at[k, pl.ds(source * blocks, blocks)]
        return pltpu.make_async_remote_copy(
            src_ref=part,
            dst_ref=part,
            send_sem=send_sem.at[k, source],
            recv_sem=low_recv.at[k, source],
            device_id=device_id,
            device_id_type=MESH,
        )

    def up(k, source):
        return low_copy(k, source, low_up, {"row": lax.rem(me + y_count, row_count)})

    def down(k, source):
        return low_copy(k, source, low_down, {"row": lax.rem(me - y_count + row_count, row_count)})

    def across(k, source):
        return low_copy(k, source, low_over, over)

    def gather(k):
        not_top = here_z + 1 < z_count
        not_bottom = here_z > 0

        @pl.when(not_top)
        def _():
            up(k, me).start()

        @pl.when(not_bottom)
        def _():
            down(k, me).start()

        if y_count > 1:
            across(k, me).start()
        for step in range(1, z_count):
            lower = me - step * y_count
            upper = me + step * y_count

            @pl.when(here_z - step >= 0)
            def _():
                up(k, lower).wait_recv()

                @pl.when(not_top)
                def _():
                    up(k, lower).start()

                if y_count > 1:
                    across(k, lower).start()

            @pl.when(here_z + step < z_count)
            def _():
                down(k, upper).wait_recv()

                @pl.when(not_bottom)
                def _():
                    down(k, upper).start()

                if y_count > 1:
                    across(k, upper).start()

        if y_count > 1:
            for z in range(z_count):
                across(k, z * y_count + (1 - here_y)).wait_recv()

    def gather_sent(k):
        for z in range(z_count):
            source = z * y_count + here_y
            if y_count > 1:
                across(k, source).wait_send()

            @pl.when((here_z >= z) & (here_z + 1 < z_count))
            def _():
                up(k, source).wait_send()

            @pl.when((here_z <= z) & (here_z > 0))
            def _():
                down(k, source).wait_send()

    def simple_copy(source, target, send_sem, recv_sem, device_id):
        return pltpu.make_async_remote_copy(
            src_ref=source,
            dst_ref=target,
            send_sem=send_sem,
            recv_sem=recv_sem,
            device_id=device_id,
            device_id_type=MESH,
        )

    def core_copy(buffer, index):
        return simple_copy(
            buffer.at[0], buffer.at[1], core_send.at[index], core_recv.at[index], sibling
        )

    def y_copy(buffer, index):
        return simple_copy(buffer.at[0], buffer.at[1], y_send.at[index], y_recv.at[index], over)

    def z_copies(buffer, index, sending):
        copies = []
        for step in range(1, z_count):
            other = lax.rem(here_z + step, z_count)
            slot = here_z if sending else other
            copies.append(
                simple_copy(
                    buffer.at[slot],
                    buffer.at[slot],
                    z_send.at[index, other],
                    z_recv.at[index, slot],
                    {"row": other * y_count + here_y},
                )
            )
        return copies

    def after_core(index, sums, y_buffer, z_buffer):
        core_copy(sums, index).wait()
        total = sums[0] + sums[1]
        if y_count > 1:
            y_buffer[0] = total
            y_copy(y_buffer, index).start()
        else:
            z_buffer[here_z] = total
            for copy in z_copies(z_buffer, index, True):
                copy.start()

    def after_y(index, y_buffer, z_buffer):
        if y_count > 1:
            y_copy(y_buffer, index).wait()
            z_buffer[here_z] = y_buffer[0] + y_buffer[1]
            for copy in z_copies(z_buffer, index, True):
                copy.start()

    def after_z(index, z_buffer):
        for copy in z_copies(z_buffer, index, False):
            copy.wait_recv()
        total = z_buffer[0]
        for z in range(1, z_count):
            total = total + z_buffer[z]
        return total

    def z_sent(index, z_buffer):
        for copy in z_copies(z_buffer, index, True):
            copy.wait_send()

    live = count_ref[0]
    band_first = me * band

    for k in range(ITERS):
        gather(k)
        partial[...] = jnp.zeros_like(partial)

        def multiply(s, carry):
            tile_col = col_ref[s]
            owner = lax.div(lax.div(tile_col, blocks), 2)
            place = owner * blocks + lax.rem(tile_col, blocks)
            product = lax.dot_general(
                gathered[k, place], tiles[s], NT, preferred_element_type=jnp.float32
            )
            mine = jnp.where(s < live, row_ref[s] - band_first, -1)
            for t in range(band):
                weight = jnp.where(mine == t, 1.0, 0.0).astype(jnp.float32)
                partial[t] += product * weight
            return carry

        if k == 0:
            for load in loads:
                load.wait()
        lax.fori_loop(0, slots, multiply, 0, unroll=2)

        cross = simple_copy(
            partial.at[pl.ds((1 - core) * blocks, blocks)],
            crossed.at[k],
            cross_send.at[k],
            cross_recv.at[k],
            sibling,
        )
        cross.start()
        gather_sent(k)
        cross.wait()
        gram = jnp.zeros((width, width), jnp.float32)
        for b in range(blocks):
            image[b] = partial[core * blocks + b] + crossed[k, b]
            gram = gram + lax.dot_general(
                image[b], image[b], NT, precision=EXACT, preferred_element_type=jnp.float32
            )
        core_sum[k, 0] = pack(gram)
        core_copy(core_sum.at[k], k).start()
        quotient = jnp.zeros((width, width), jnp.float32)
        for b in range(blocks):
            quotient = quotient + lax.dot_general(
                iterate[b], image[b], NT, precision=EXACT, preferred_element_type=jnp.float32
            )
        rit_core[0, k] = pack(quotient)
        last = k == ITERS - 1
        if last:
            core_copy(rit_core, ITERS).start()
        after_core(k, core_sum.at[k], y_sum.at[k], z_sum.at[k])
        if last:
            after_core(ITERS, rit_core, rit_y, rit_z)
        after_y(k, y_sum.at[k], z_sum.at[k])
        if last:
            after_y(ITERS, rit_y, rit_z)
        total = after_z(k, z_sum.at[k])
        inverse = inverse_factor(unpack(total) * (1.0 / nodes), work, scale)
        for b in range(blocks):
            fresh = lax.dot_general(
                inverse,
                image[b],
                (((1,), (0,)), ((), ())),
                precision=EXACT,
                preferred_element_type=jnp.float32,
            )
            if last:
                basis_ref[b * TILE : (b + 1) * TILE, :] = fresh.T
            else:
                iterate[b] = fresh
                gathered[k + 1, me * blocks + b] = fresh.astype(jnp.bfloat16)
        z_sent(k, z_sum.at[k])
    total = after_z(ITERS, rit_z)
    z_sent(ITERS, rit_z)
    for k in range(ITERS):
        ritz_ref[k] = unpack(total[k]) * (float(nodes) ** -0.5)


def per_device(tiles, tile_row, tile_col, counts, start):
    row_count = lax.axis_size("row")
    col_count = lax.axis_size("col")
    y_count = 2 if row_count == 8 else 1
    z_count = row_count // y_count
    blocks = start.shape[0] // TILE
    width = start.shape[1]
    nodes = start.shape[0] * row_count * col_count
    half = (width // 2, 2 * width)
    dma = pltpu.SemaphoreType.DMA
    vmem = pl.BlockSpec(memory_space=pltpu.VMEM)
    smem = pl.BlockSpec(memory_space=pltpu.SMEM)
    return pl.pallas_call(
        functools.partial(kernel, row_count, y_count, nodes),
        out_shape=(
            jax.ShapeDtypeStruct(start.shape, jnp.float32),
            jax.ShapeDtypeStruct((ITERS, width, width), jnp.float32),
        ),
        in_specs=[pl.BlockSpec(memory_space=pl.ANY), smem, smem, smem, vmem],
        out_specs=(vmem, vmem),
        scratch_shapes=[
            pltpu.VMEM(tiles.shape, jnp.bfloat16),
            pltpu.VMEM((ITERS, row_count * blocks, width, TILE), jnp.bfloat16),
            pltpu.VMEM((col_count * blocks, width, TILE), jnp.float32),
            pltpu.VMEM((ITERS, blocks, width, TILE), jnp.float32),
            pltpu.VMEM((blocks, width, TILE), jnp.float32),
            pltpu.VMEM((blocks, width, TILE), jnp.float32),
            pltpu.VMEM((ITERS, 2) + half, jnp.float32),
            pltpu.VMEM((ITERS, 2) + half, jnp.float32),
            pltpu.VMEM((ITERS, z_count) + half, jnp.float32),
            pltpu.VMEM((2, ITERS) + half, jnp.float32),
            pltpu.VMEM((2, ITERS) + half, jnp.float32),
            pltpu.VMEM((z_count, ITERS) + half, jnp.float32),
            pltpu.VMEM((width, 2 * width), jnp.float32),
            pltpu.VMEM((width, 2 * width), jnp.float32),
            dma((LOADS,)),
            dma((ITERS, row_count)),
            dma((ITERS, row_count)),
            dma((ITERS, row_count)),
            dma((ITERS, row_count)),
            dma((ITERS,)),
            dma((ITERS,)),
            dma((ITERS + 1,)),
            dma((ITERS + 1,)),
            dma((ITERS + 1,)),
            dma((ITERS + 1,)),
            dma((ITERS + 1, z_count)),
            dma((ITERS + 1, z_count)),
        ],
        compiler_params=pltpu.CompilerParams(
            collective_id=0, has_side_effects=True, vmem_limit_bytes=56 * 1024 * 1024
        ),
    )(tiles, tile_row, tile_col, counts, start)


def solution(mesh):
    return jax.shard_map(
        per_device,
        mesh=mesh,
        in_specs=(
            P(("grp", "row", "col"), None, None),
            P(("grp", "row", "col")),
            P(("grp", "row", "col")),
            P(("grp", "row", "col")),
            P(("grp", "row", "col"), None),
        ),
        out_specs=(P(("grp", "row", "col"), None), P("grp", None, None)),
        check_vma=False,
    )
```

```python
import functools

import jax
import jax.numpy as jnp
from jax import lax
from jax.experimental import pallas as pl
from jax.experimental.pallas import tpu as pltpu
from jax.sharding import PartitionSpec as P

TILE = 512
ITERS = 3
MESH = pl.DeviceIdType.MESH
EXACT = lax.Precision.HIGHEST
NT = (((1,), (1,)), ((), ()))
LOADS = 4
PARTS = 2
EXTRA = 2


def pack(square):
    half = square.shape[0] // 2
    return jnp.concatenate([square[:half], square[half:]], axis=1)


def unpack(packed):
    half = packed.shape[1] // 2
    return jnp.concatenate([packed[:, :half], packed[:, half:]], axis=0)


def inverse_factor(gram, work, scale):
    width = gram.shape[0]
    lanes = 2 * width
    rows = lax.broadcasted_iota(jnp.int32, (width, lanes), 0)
    columns = lax.broadcasted_iota(jnp.int32, (width, lanes), 1)
    rows8 = lax.broadcasted_iota(jnp.int32, (8, lanes), 0)
    eye = (rows + width == columns).astype(jnp.float32)
    padded = jnp.concatenate([gram, jnp.zeros_like(gram)], axis=1)
    work[...] = padded + eye

    def body(block, carry):
        whole = work[...]
        first = pl.multiple_of(block * 8, 8)
        here = work[pl.ds(first, 8), :]
        below = rows - first
        cols = [jnp.broadcast_to(whole[:, q : q + 1], (width, lanes)) for q in range(8)]
        cols8 = [jnp.broadcast_to(here[:, q : q + 1], (8, lanes)) for q in range(8)]
        pivots = jnp.ones((8, lanes), jnp.float32)
        for p in range(8):
            inverse = 1.0 / cols8[p][p : p + 1, :]
            pivots = jnp.where(rows8 == p, inverse, pivots)
            factor = jnp.where(below > p, cols[p] * inverse, 0.0)
            factor8 = jnp.where(rows8 > p, cols8[p] * inverse, 0.0)
            pivot_row = here[p : p + 1, :]
            for q in range(p + 1, 8):
                entry = cols8[q][p : p + 1, :]
                cols[q] = cols[q] - factor * entry
                cols8[q] = cols8[q] - factor8 * entry
            here = here - factor8 * pivot_row
            whole = whole - factor * pivot_row
        scale[pl.ds(first, 8), :] = pivots
        work[...] = pltpu.roll(whole, lanes - 8, 1)
        return carry

    lax.fori_loop(0, width // 8, body, 0)
    return (work[...] * jnp.sqrt(scale[...]))[:, :width]


def kernel(
    row_count,
    y_count,
    nodes,
    tiles_hbm,
    row_ref,
    col_ref,
    count_ref,
    start_ref,
    basis_ref,
    ritz_ref,
    tiles,
    gathered,
    partial,
    crossed,
    image,
    iterate,
    core_sum,
    row_sum,
    work,
    scale,
    load_sem,
    low_recv,
    low_up,
    low_down,
    low_over,
    cross_send,
    cross_recv,
    core_send,
    core_recv,
    row_send,
    row_recv,
):
    z_count = row_count // y_count
    me = lax.axis_index("row")
    core = lax.axis_index("col")
    here_z = me // y_count
    here_y = me % y_count
    blocks = iterate.shape[0]
    width = iterate.shape[1]
    slots = tiles.shape[0]
    band = partial.shape[0]
    sibling = {"col": 1 - core}
    over = {"row": here_z * y_count + (1 - here_y)}

    chunk = slots // LOADS
    loads = [
        pltpu.make_async_copy(
            tiles_hbm.at[pl.ds(i * chunk, chunk)],
            tiles.at[pl.ds(i * chunk, chunk)],
            load_sem.at[i],
        )
        for i in range(LOADS)
    ]
    for load in loads:
        load.start()

    barrier = pltpu.get_barrier_semaphore()
    pl.semaphore_signal(barrier, inc=1, device_id=sibling, device_id_type=MESH)
    for step in range(1, row_count):
        other = lax.rem(me + step, row_count)
        pl.semaphore_signal(barrier, inc=1, device_id={"row": other}, device_id_type=MESH)

    for b in range(blocks):
        iterate[b] = start_ref[:, b * TILE : (b + 1) * TILE]
        gathered[0, me * blocks + b] = iterate[b].astype(jnp.bfloat16)
    pl.semaphore_wait(barrier, row_count)

    not_top = here_z + 1 < z_count
    not_bottom = here_z > 0

    def at_end(z):
        return y_count > 1 and z in (0, z_count - 1)

    pieces = blocks * PARTS
    piece_rows = width // PARTS

    def low_copy(k, item, send_sem, device_id):
        z, y, q = item
        row = z * y_count + y
        piece = gathered.at[
            k, row * blocks + q // PARTS, pl.ds(q % PARTS * piece_rows, piece_rows)
        ]
        flag = row * pieces + q
        return pltpu.make_async_remote_copy(
            src_ref=piece,
            dst_ref=piece,
            send_sem=send_sem.at[k, flag],
            recv_sem=low_recv.at[k, flag],
            device_id=device_id,
            device_id_type=MESH,
        )

    def up(k, item):
        return low_copy(k, item, low_up, {"row": lax.rem(me + y_count, row_count)})

    def down(k, item):
        return low_copy(k, item, low_down, {"row": lax.rem(me - y_count + row_count, row_count)})

    def across(k, item):
        return low_copy(k, item, low_over, over)

    plain = pieces - EXTRA

    def gather(k):
        for b in reversed(range(pieces)):
            item = (here_z, here_y, b)

            @pl.when(not_top)
            def _():
                up(k, item).start()

            @pl.when(not_bottom)
            def _():
                down(k, item).start()

            if y_count > 1:
                across(k, item).start()

        if y_count > 1:
            for b in reversed(range(plain, pieces)):
                item = (here_z, 1 - here_y, b)

                @pl.when(here_z == 0)
                def _():
                    across(k, item).wait_recv()
                    up(k, item).start()

                @pl.when(here_z == z_count - 1)
                def _():
                    across(k, item).wait_recv()
                    down(k, item).start()

        for step in range(1, z_count):
            lower = here_z - step
            upper = here_z + step
            for b in reversed(range(pieces)):

                @pl.when(lower >= 0)
                def _():
                    item = (lower, here_y, b)
                    up(k, item).wait_recv()

                    @pl.when(not_top)
                    def _():
                        up(k, item).start()

                    if y_count > 1:
                        if b < plain:
                            across(k, item).start()
                        else:

                            @pl.when(lower > 0)
                            def _():
                                across(k, item).start()

                @pl.when(upper < z_count)
                def _():
                    item = (upper, here_y, b)
                    down(k, item).wait_recv()

                    @pl.when(not_bottom)
                    def _():
                        down(k, item).start()

                    if y_count > 1:
                        if b < plain:
                            across(k, item).start()
                        else:

                            @pl.when(upper < z_count - 1)
                            def _():
                                across(k, item).start()

            if y_count > 1:
                for b in reversed(range(plain, pieces)):

                    @pl.when(lower == 0)
                    def _():
                        item = (0, 1 - here_y, b)
                        up(k, item).wait_recv()

                        @pl.when(not_top)
                        def _():
                            up(k, item).start()

                    @pl.when(upper == z_count - 1)
                    def _():
                        item = (z_count - 1, 1 - here_y, b)
                        down(k, item).wait_recv()

                        @pl.when(not_bottom)
                        def _():
                            down(k, item).start()

        if y_count > 1:
            for z in range(z_count):
                for b in range(pieces):
                    if b < plain or not at_end(z):
                        across(k, (z, 1 - here_y, b)).wait_recv()

    def gather_sent(k):
        for z in range(z_count):
            for b in range(pieces):
                item = (z, here_y, b)
                extra = b >= plain and at_end(z)
                if y_count > 1:
                    if extra:

                        @pl.when(here_z == z)
                        def _():
                            across(k, item).wait_send()

                    else:
                        across(k, item).wait_send()

                @pl.when((here_z >= z) & not_top)
                def _():
                    up(k, item).wait_send()
                    if extra:
                        up(k, (z, 1 - here_y, b)).wait_send()

                @pl.when((here_z <= z) & not_bottom)
                def _():
                    down(k, item).wait_send()
                    if extra:
                        down(k, (z, 1 - here_y, b)).wait_send()

    def simple_copy(source, target, send_sem, recv_sem, device_id):
        return pltpu.make_async_remote_copy(
            src_ref=source,
            dst_ref=target,
            send_sem=send_sem,
            recv_sem=recv_sem,
            device_id=device_id,
            device_id_type=MESH,
        )

    def core_copy(i):
        return simple_copy(
            core_sum.at[i, 0], core_sum.at[i, 1], core_send.at[i], core_recv.at[i], sibling
        )

    def row_copies(i, sending):
        copies = []
        for step in range(1, row_count):
            other = lax.rem(me + step, row_count)
            slot = me if sending else other
            copies.append(
                simple_copy(
                    row_sum.at[i, slot],
                    row_sum.at[i, slot],
                    row_send.at[i, other],
                    row_recv.at[i, slot],
                    {"row": other},
                )
            )
        return copies

    def spread(i):
        core_copy(i).wait()
        row_sum[i, me] = core_sum[i, 0] + core_sum[i, 1]
        for copy in row_copies(i, True):
            copy.start()

    def collect(i):
        for copy in row_copies(i, False):
            copy.wait_recv()
        total = row_sum[i, 0]
        for r in range(1, row_count):
            total = total + row_sum[i, r]
        return unpack(total)

    def collect_ritz(k):
        ritz_ref[k] = collect(ITERS + k) * (float(nodes) ** -0.5)

    def row_sent(i):
        for copy in row_copies(i, True):
            copy.wait_send()

    live = count_ref[0]
    band_first = me * band

    for k in range(ITERS):
        gather(k)
        if k > 0:
            spread(ITERS + k - 1)
        partial[...] = jnp.zeros_like(partial)

        def multiply(s, carry):
            tile_col = col_ref[s]
            owner = lax.div(lax.div(tile_col, blocks), 2)
            place = owner * blocks + lax.rem(tile_col, blocks)
            product = lax.dot_general(
                gathered[k, place], tiles[s], NT, preferred_element_type=jnp.float32
            )
            mine = jnp.where(s < live, row_ref[s] - band_first, -1)
            for t in range(band):
                weight = jnp.where(mine == t, 1.0, 0.0).astype(jnp.float32)
                partial[t] += product * weight
            return carry

        if k == 0:
            for load in loads:
                load.wait()
        lax.fori_loop(0, slots, multiply, 0, unroll=4)

        cross = simple_copy(
            partial.at[pl.ds((1 - core) * blocks, blocks)],
            crossed.at[k],
            cross_send.at[k],
            cross_recv.at[k],
            sibling,
        )
        cross.start()
        gather_sent(k)
        if k > 0:
            collect_ritz(k - 1)
            row_sent(ITERS + k - 1)
        cross.wait()
        gram = jnp.zeros((width, width), jnp.float32)
        for b in range(blocks):
            image[b] = partial[core * blocks + b] + crossed[k, b]
            gram = gram + lax.dot_general(
                image[b], image[b], NT, precision=EXACT, preferred_element_type=jnp.float32
            )
        core_sum[k, 0] = pack(gram)
        core_copy(k).start()
        quotient = jnp.zeros((width, width), jnp.float32)
        for b in range(blocks):
            quotient = quotient + lax.dot_general(
                iterate[b], image[b], NT, precision=EXACT, preferred_element_type=jnp.float32
            )
        core_sum[ITERS + k, 0] = pack(quotient)
        last = k == ITERS - 1
        core_copy(ITERS + k).start()
        spread(k)
        if last:
            spread(ITERS + k)
        inverse = inverse_factor(collect(k) * (1.0 / nodes), work, scale)
        for b in range(blocks):
            fresh = lax.dot_general(
                inverse,
                image[b],
                (((1,), (0,)), ((), ())),
                precision=EXACT,
                preferred_element_type=jnp.float32,
            )
            if last:
                basis_ref[:, b * TILE : (b + 1) * TILE] = fresh
            else:
                iterate[b] = fresh
                gathered[k + 1, me * blocks + b] = fresh.astype(jnp.bfloat16)
        row_sent(k)
    collect_ritz(ITERS - 1)
    row_sent(2 * ITERS - 1)


def per_device(tiles, tile_row, tile_col, counts, start):
    row_count = lax.axis_size("row")
    col_count = lax.axis_size("col")
    y_count = 2 if row_count == 8 else 1
    z_count = row_count // y_count
    blocks = start.shape[0] // TILE
    width = start.shape[1]
    nodes = start.shape[0] * row_count * col_count
    half = (width // 2, 2 * width)
    dma = pltpu.SemaphoreType.DMA
    vmem = pl.BlockSpec(memory_space=pltpu.VMEM)
    smem = pl.BlockSpec(memory_space=pltpu.SMEM)
    basis, ritz = pl.pallas_call(
        functools.partial(kernel, row_count, y_count, nodes),
        out_shape=(
            jax.ShapeDtypeStruct((width, start.shape[0]), jnp.float32),
            jax.ShapeDtypeStruct((ITERS, width, width), jnp.float32),
        ),
        in_specs=[pl.BlockSpec(memory_space=pl.ANY), smem, smem, smem, vmem],
        out_specs=(vmem, vmem),
        scratch_shapes=[
            pltpu.VMEM(tiles.shape, jnp.bfloat16),
            pltpu.VMEM((ITERS, row_count * blocks, width, TILE), jnp.bfloat16),
            pltpu.VMEM((col_count * blocks, width, TILE), jnp.float32),
            pltpu.VMEM((ITERS, blocks, width, TILE), jnp.float32),
            pltpu.VMEM((blocks, width, TILE), jnp.float32),
            pltpu.VMEM((blocks, width, TILE), jnp.float32),
            pltpu.VMEM((2 * ITERS, 2) + half, jnp.float32),
            pltpu.VMEM((2 * ITERS, row_count) + half, jnp.float32),
            pltpu.VMEM((width, 2 * width), jnp.float32),
            pltpu.VMEM((width, 2 * width), jnp.float32),
            dma((LOADS,)),
            dma((ITERS, row_count * blocks * PARTS)),
            dma((ITERS, row_count * blocks * PARTS)),
            dma((ITERS, row_count * blocks * PARTS)),
            dma((ITERS, row_count * blocks * PARTS)),
            dma((ITERS,)),
            dma((ITERS,)),
            dma((2 * ITERS,)),
            dma((2 * ITERS,)),
            dma((2 * ITERS, row_count)),
            dma((2 * ITERS, row_count)),
        ],
        compiler_params=pltpu.CompilerParams(
            collective_id=0, has_side_effects=True, vmem_limit_bytes=56 * 1024 * 1024
        ),
    )(tiles, tile_row, tile_col, counts, start.T)
    return basis.T, ritz


def solution(mesh):
    return jax.shard_map(
        per_device,
        mesh=mesh,
        in_specs=(
            P(("grp", "row", "col"), None, None),
            P(("grp", "row", "col")),
            P(("grp", "row", "col")),
            P(("grp", "row", "col")),
            P(("grp", "row", "col"), None),
        ),
        out_specs=(P(("grp", "row", "col"), None), P("grp", None, None)),
        check_vma=False,
    )
```

```python
import functools

import jax
import jax.numpy as jnp
from jax import lax
from jax.experimental import pallas as pl
from jax.experimental.pallas import tpu as pltpu
from jax.sharding import PartitionSpec as P

TILE = 512
ITERS = 3
MESH = pl.DeviceIdType.MESH
EXACT = lax.Precision.HIGHEST
NT = (((1,), (1,)), ((), ()))
LOADS = 4
PARTS = 2
EXTRA = 2


def pack(square):
    half = square.shape[0] // 2
    return jnp.concatenate([square[:half], square[half:]], axis=1)


def unpack(packed):
    half = packed.shape[1] // 2
    return jnp.concatenate([packed[:, :half], packed[:, half:]], axis=0)


def inverse_factor(gram, work, scale):
    width = gram.shape[0]
    lanes = 2 * width
    rows = lax.broadcasted_iota(jnp.int32, (width, lanes), 0)
    columns = lax.broadcasted_iota(jnp.int32, (width, lanes), 1)
    rows8 = lax.broadcasted_iota(jnp.int32, (8, lanes), 0)
    eye = (rows + width == columns).astype(jnp.float32)
    padded = jnp.concatenate([gram, jnp.zeros_like(gram)], axis=1)
    work[...] = padded + eye

    def body(block, carry):
        whole = work[...]
        first = pl.multiple_of(block * 8, 8)
        here = work[pl.ds(first, 8), :]
        below = rows - first
        cols = [jnp.broadcast_to(whole[:, q : q + 1], (width, lanes)) for q in range(8)]
        cols8 = [jnp.broadcast_to(here[:, q : q + 1], (8, lanes)) for q in range(8)]
        pivots = jnp.ones((8, lanes), jnp.float32)
        for p in range(8):
            inverse = 1.0 / cols8[p][p : p + 1, :]
            pivots = jnp.where(rows8 == p, inverse, pivots)
            factor = jnp.where(below > p, cols[p] * inverse, 0.0)
            factor8 = jnp.where(rows8 > p, cols8[p] * inverse, 0.0)
            pivot_row = here[p : p + 1, :]
            for q in range(p + 1, 8):
                entry = cols8[q][p : p + 1, :]
                cols[q] = cols[q] - factor * entry
                cols8[q] = cols8[q] - factor8 * entry
            here = here - factor8 * pivot_row
            whole = whole - factor * pivot_row
        scale[pl.ds(first, 8), :] = pivots
        work[...] = pltpu.roll(whole, lanes - 8, 1)
        return carry

    lax.fori_loop(0, width // 8, body, 0)
    return (work[...] * jnp.sqrt(scale[...]))[:, :width]


def kernel(
    row_count,
    y_count,
    nodes,
    tiles_hbm,
    row_ref,
    col_ref,
    count_ref,
    start_ref,
    basis_ref,
    ritz_ref,
    tiles,
    gathered,
    partial,
    crossed,
    image,
    iterate,
    core_sum,
    row_sum,
    work,
    scale,
    load_sem,
    low_recv,
    low_up,
    low_down,
    low_over,
    cross_send,
    cross_recv,
    core_send,
    core_recv,
    row_send,
    row_recv,
):
    z_count = row_count // y_count
    me = lax.axis_index("row")
    core = lax.axis_index("col")
    here_z = me // y_count
    here_y = me % y_count
    blocks = iterate.shape[0]
    width = iterate.shape[1]
    slots = tiles.shape[0]
    band = partial.shape[0]
    sibling = {"col": 1 - core}
    over = {"row": here_z * y_count + (1 - here_y)}

    chunk = slots // LOADS
    loads = [
        pltpu.make_async_copy(
            tiles_hbm.at[pl.ds(i * chunk, chunk)],
            tiles.at[pl.ds(i * chunk, chunk)],
            load_sem.at[i],
        )
        for i in range(LOADS)
    ]
    for load in loads:
        load.start()

    barrier = pltpu.get_barrier_semaphore()
    pl.semaphore_signal(barrier, inc=1, device_id=sibling, device_id_type=MESH)
    for step in range(1, row_count):
        other = lax.rem(me + step, row_count)
        pl.semaphore_signal(barrier, inc=1, device_id={"row": other}, device_id_type=MESH)

    for b in range(blocks):
        iterate[b] = start_ref[:, b * TILE : (b + 1) * TILE]
        gathered[0, me * blocks + b] = iterate[b].astype(jnp.bfloat16)
    pl.semaphore_wait(barrier, row_count)

    not_top = here_z + 1 < z_count
    not_bottom = here_z > 0

    def at_end(z):
        return y_count > 1 and z in (0, z_count - 1)

    pieces = blocks * PARTS
    piece_rows = width // PARTS

    def low_copy(k, item, send_sem, device_id):
        z, y, q = item
        row = z * y_count + y
        piece = gathered.at[
            k, row * blocks + q // PARTS, pl.ds(q % PARTS * piece_rows, piece_rows)
        ]
        flag = row * pieces + q
        return pltpu.make_async_remote_copy(
            src_ref=piece,
            dst_ref=piece,
            send_sem=send_sem.at[k, flag],
            recv_sem=low_recv.at[k, flag],
            device_id=device_id,
            device_id_type=MESH,
        )

    def up(k, item):
        return low_copy(k, item, low_up, {"row": lax.rem(me + y_count, row_count)})

    def down(k, item):
        return low_copy(k, item, low_down, {"row": lax.rem(me - y_count + row_count, row_count)})

    def across(k, item):
        return low_copy(k, item, low_over, over)

    plain = pieces - EXTRA

    def gather(k):
        for b in reversed(range(pieces)):
            item = (here_z, here_y, b)

            @pl.when(not_top)
            def _():
                up(k, item).start()

            @pl.when(not_bottom)
            def _():
                down(k, item).start()

            if y_count > 1:
                across(k, item).start()

        if y_count > 1:
            for b in reversed(range(plain, pieces)):
                item = (here_z, 1 - here_y, b)

                @pl.when(here_z == 0)
                def _():
                    across(k, item).wait_recv()
                    up(k, item).start()

                @pl.when(here_z == z_count - 1)
                def _():
                    across(k, item).wait_recv()
                    down(k, item).start()

        for step in range(1, z_count):
            lower = here_z - step
            upper = here_z + step
            for b in reversed(range(pieces)):

                @pl.when(lower >= 0)
                def _():
                    item = (lower, here_y, b)
                    up(k, item).wait_recv()

                    @pl.when(not_top)
                    def _():
                        up(k, item).start()

                    if y_count > 1:
                        if b < plain:
                            across(k, item).start()
                        else:

                            @pl.when(lower > 0)
                            def _():
                                across(k, item).start()

                @pl.when(upper < z_count)
                def _():
                    item = (upper, here_y, b)
                    down(k, item).wait_recv()

                    @pl.when(not_bottom)
                    def _():
                        down(k, item).start()

                    if y_count > 1:
                        if b < plain:
                            across(k, item).start()
                        else:

                            @pl.when(upper < z_count - 1)
                            def _():
                                across(k, item).start()

            if y_count > 1:
                for b in reversed(range(plain, pieces)):

                    @pl.when(lower == 0)
                    def _():
                        item = (0, 1 - here_y, b)
                        up(k, item).wait_recv()

                        @pl.when(not_top)
                        def _():
                            up(k, item).start()

                    @pl.when(upper == z_count - 1)
                    def _():
                        item = (z_count - 1, 1 - here_y, b)
                        down(k, item).wait_recv()

                        @pl.when(not_bottom)
                        def _():
                            down(k, item).start()

        if y_count > 1:
            for z in range(z_count):
                for b in range(pieces):
                    if b < plain or not at_end(z):
                        across(k, (z, 1 - here_y, b)).wait_recv()

    def gather_sent(k):
        for z in range(z_count):
            for b in range(pieces):
                item = (z, here_y, b)
                extra = b >= plain and at_end(z)
                if y_count > 1:
                    if extra:

                        @pl.when(here_z == z)
                        def _():
                            across(k, item).wait_send()

                    else:
                        across(k, item).wait_send()

                @pl.when((here_z >= z) & not_top)
                def _():
                    up(k, item).wait_send()
                    if extra:
                        up(k, (z, 1 - here_y, b)).wait_send()

                @pl.when((here_z <= z) & not_bottom)
                def _():
                    down(k, item).wait_send()
                    if extra:
                        down(k, (z, 1 - here_y, b)).wait_send()

    def simple_copy(source, target, send_sem, recv_sem, device_id):
        return pltpu.make_async_remote_copy(
            src_ref=source,
            dst_ref=target,
            send_sem=send_sem,
            recv_sem=recv_sem,
            device_id=device_id,
            device_id_type=MESH,
        )

    def core_copy(i):
        return simple_copy(
            core_sum.at[i, 0], core_sum.at[i, 1], core_send.at[i], core_recv.at[i], sibling
        )

    def row_copies(i, sending):
        copies = []
        for step in range(1, row_count):
            other = lax.rem(me + step, row_count)
            slot = me if sending else other
            copies.append(
                simple_copy(
                    row_sum.at[i, slot],
                    row_sum.at[i, slot],
                    row_send.at[i, other],
                    row_recv.at[i, slot],
                    {"row": other},
                )
            )
        return copies

    def spread(i):
        core_copy(i).wait()
        row_sum[i, me] = core_sum[i, 0] + core_sum[i, 1]
        for copy in row_copies(i, True):
            copy.start()

    def collect(i):
        for copy in row_copies(i, False):
            copy.wait_recv()
        total = row_sum[i, 0]
        for r in range(1, row_count):
            total = total + row_sum[i, r]
        return unpack(total)

    def collect_ritz(k):
        ritz_ref[k] = collect(ITERS + k) * (float(nodes) ** -0.5)

    def row_sent(i):
        for copy in row_copies(i, True):
            copy.wait_send()

    live = count_ref[0]
    band_first = me * band

    for k in range(ITERS):
        gather(k)
        if k > 0:
            spread(ITERS + k - 1)
        partial[...] = jnp.zeros_like(partial)

        def multiply(s, carry):
            tile_col = col_ref[s]
            owner = lax.div(lax.div(tile_col, blocks), 2)
            place = owner * blocks + lax.rem(tile_col, blocks)
            product = lax.dot_general(
                gathered[k, place], tiles[s], NT, preferred_element_type=jnp.float32
            )
            mine = jnp.where(s < live, row_ref[s] - band_first, -1)
            for t in range(band):
                weight = jnp.where(mine == t, 1.0, 0.0).astype(jnp.float32)
                partial[t] += product * weight
            return carry

        if k == 0:
            for load in loads:
                load.wait()
        lax.fori_loop(0, slots, multiply, 0, unroll=8)

        cross = simple_copy(
            partial.at[pl.ds((1 - core) * blocks, blocks)],
            crossed.at[k],
            cross_send.at[k],
            cross_recv.at[k],
            sibling,
        )
        cross.start()
        gather_sent(k)
        if k > 0:
            collect_ritz(k - 1)
            row_sent(ITERS + k - 1)
        cross.wait()
        gram = jnp.zeros((width, width), jnp.float32)
        for b in range(blocks):
            image[b] = partial[core * blocks + b] + crossed[k, b]
            gram = gram + lax.dot_general(
                image[b], image[b], NT, precision=EXACT, preferred_element_type=jnp.float32
            )
        core_sum[k, 0] = pack(gram)
        core_copy(k).start()
        quotient = jnp.zeros((width, width), jnp.float32)
        for b in range(blocks):
            quotient = quotient + lax.dot_general(
                iterate[b], image[b], NT, precision=EXACT, preferred_element_type=jnp.float32
            )
        core_sum[ITERS + k, 0] = pack(quotient)
        last = k == ITERS - 1
        core_copy(ITERS + k).start()
        spread(k)
        if last:
            spread(ITERS + k)
        inverse = inverse_factor(collect(k) * (1.0 / nodes), work, scale)
        for b in range(blocks):
            fresh = lax.dot_general(
                inverse,
                image[b],
                (((1,), (0,)), ((), ())),
                precision=EXACT,
                preferred_element_type=jnp.float32,
            )
            if last:
                basis_ref[:, b * TILE : (b + 1) * TILE] = fresh
            else:
                iterate[b] = fresh
                gathered[k + 1, me * blocks + b] = fresh.astype(jnp.bfloat16)
        row_sent(k)
    collect_ritz(ITERS - 1)
    row_sent(2 * ITERS - 1)


def per_device(tiles, tile_row, tile_col, counts, start):
    row_count = lax.axis_size("row")
    col_count = lax.axis_size("col")
    y_count = 2 if row_count == 8 else 1
    z_count = row_count // y_count
    blocks = start.shape[0] // TILE
    width = start.shape[1]
    nodes = start.shape[0] * row_count * col_count
    half = (width // 2, 2 * width)
    dma = pltpu.SemaphoreType.DMA
    vmem = pl.BlockSpec(memory_space=pltpu.VMEM)
    smem = pl.BlockSpec(memory_space=pltpu.SMEM)
    basis, ritz = pl.pallas_call(
        functools.partial(kernel, row_count, y_count, nodes),
        out_shape=(
            jax.ShapeDtypeStruct((width, start.shape[0]), jnp.float32),
            jax.ShapeDtypeStruct((ITERS, width, width), jnp.float32),
        ),
        in_specs=[pl.BlockSpec(memory_space=pl.ANY), smem, smem, smem, vmem],
        out_specs=(vmem, vmem),
        scratch_shapes=[
            pltpu.VMEM(tiles.shape, jnp.bfloat16),
            pltpu.VMEM((ITERS, row_count * blocks, width, TILE), jnp.bfloat16),
            pltpu.VMEM((col_count * blocks, width, TILE), jnp.float32),
            pltpu.VMEM((ITERS, blocks, width, TILE), jnp.float32),
            pltpu.VMEM((blocks, width, TILE), jnp.float32),
            pltpu.VMEM((blocks, width, TILE), jnp.float32),
            pltpu.VMEM((2 * ITERS, 2) + half, jnp.float32),
            pltpu.VMEM((2 * ITERS, row_count) + half, jnp.float32),
            pltpu.VMEM((width, 2 * width), jnp.float32),
            pltpu.VMEM((width, 2 * width), jnp.float32),
            dma((LOADS,)),
            dma((ITERS, row_count * blocks * PARTS)),
            dma((ITERS, row_count * blocks * PARTS)),
            dma((ITERS, row_count * blocks * PARTS)),
            dma((ITERS, row_count * blocks * PARTS)),
            dma((ITERS,)),
            dma((ITERS,)),
            dma((2 * ITERS,)),
            dma((2 * ITERS,)),
            dma((2 * ITERS, row_count)),
            dma((2 * ITERS, row_count)),
        ],
        compiler_params=pltpu.CompilerParams(
            collective_id=0, has_side_effects=True, vmem_limit_bytes=56 * 1024 * 1024
        ),
    )(tiles, tile_row, tile_col, counts, start.T)
    return basis.T, ritz


def solution(mesh):
    return jax.shard_map(
        per_device,
        mesh=mesh,
        in_specs=(
            P(("grp", "row", "col"), None, None),
            P(("grp", "row", "col")),
            P(("grp", "row", "col")),
            P(("grp", "row", "col")),
            P(("grp", "row", "col"), None),
        ),
        out_specs=(P(("grp", "row", "col"), None), P("grp", None, None)),
        check_vma=False,
    )
```
